32 devices in a mesh: grp: 2 (over y), row: 8 (over z, x), blk: 2 (over core).
Axes of the slice: x: 2, y: 2, z: 4, core: 2. Of those that a mesh axis runs over, the one named last changes fastest.
Arguments:
- density: float32 [64, 5, 128, 128], P(('grp', 'row'), None, 'blk'), parts along dimension 0, may hold values from -1 to 2, as said below
- pattern: int32 [64, 5], P(('grp', 'row')), parts along dimension 0, may hold values from 0 to 1, as said below
Outputs:
- purified: float32 [64, 5, 128, 128], P(('grp', 'row'), None, 'blk'), parts along dimension 0
- occupancy: float32 [4], P('grp'), parts along dimension 0
The draws below stay inside these ranges and needn't reach their ends.
There are 2 independent parts, one for each index of `grp`. The reference program is written for one: setup_inputs(seed, part) draws one part's arguments, and reference() takes and returns one part's arrays. A program takes and returns all parts, laid end to end along the dimension named above; each array names one. Nothing has to cross between parts.
Inputs may be any that keep to these rules, and one draw needn't show every extreme that they name: pattern[i, 2] = 1 and pattern[i, 2 + o] = pattern[(i + o) mod 32, 2 - o]. `density`: zero in every block whose pattern entry is 0; block (i, 2 + o) is the transpose of block ((i + o) mod 32, 2 - o).
All inputs are finite; a program needn't handle non-finite values.
Results may differ from the reference program's by a relative error of at most 0.00016.
Values sent between devices are 32-bit elements; how exact they have to be, the bound alone decides.
A program may use at most 64 MiB of HBM per device.

```python
import jax
import jax.numpy as jnp
from jax import lax

B = 128
W = 2
ITERS = 2
R = 4
K = 5
NB = 32


def pattern_shared(key):
    base = jax.random.fold_in(key, 11)
    levels = jax.random.randint(jax.random.fold_in(base, 1), (NB // R,), 1, 9)
    levels = jnp.repeat(levels, R)
    raw = jax.random.randint(jax.random.fold_in(base, 2), (NB, W), 0, 8)
    bits = (raw < levels[:, None]).astype(jnp.int32)
    columns = [None] * K
    columns[W] = jnp.ones((NB,), jnp.int32)
    for offset in range(1, W + 1):
        columns[W + offset] = bits[:, offset - 1]
        columns[W - offset] = jnp.roll(bits[:, offset - 1], offset, axis=0)
    return jnp.stack(columns, axis=1)


def draw_pattern(key, part):
    return pattern_shared(key)


def draw_density(key, part):
    mask = pattern_shared(key)
    shift_key = jax.random.fold_in(key, 7)
    key = jax.random.fold_in(key, 5)
    noise = 0.012 * jnp.clip(jax.random.normal(key, (NB, K, B, B), jnp.float32), -4.0, 4.0)
    lifted = jax.random.uniform(shift_key, (NB, B), jnp.float32, 0.0, 0.1)
    eye = jnp.eye(B, dtype=jnp.float32)
    blocks = [None] * K
    center = noise[:, W]
    blocks[W] = (0.5 * eye)[None] + eye[None] * lifted[:, :, None] + (center + jnp.swapaxes(center, 1, 2)) * 0.7071
    for offset in range(1, W + 1):
        blocks[W + offset] = noise[:, W + offset]
        blocks[W - offset] = jnp.swapaxes(jnp.roll(noise[:, W + offset], offset, axis=0), 1, 2)
    full = jnp.stack(blocks, axis=1)
    return full * mask.astype(jnp.float32)[:, :, None, None]


def setup_inputs(seed: int = 0, part: int = 0) -> dict:
    streams_of = jax.random.split(jax.random.key(seed), 3)
    part_splits = jax.random.split(jax.random.fold_in(streams_of[2], part), 3)
    return {
        "density": draw_density(jax.random.fold_in(jax.random.fold_in(streams_of[2], part), 71), part),
        "pattern": draw_pattern(jax.random.fold_in(jax.random.fold_in(streams_of[2], part), 71), part),
    }


def block_product(left, right, pattern):
    rows = left.shape[0]
    blocks = []
    for out_off in range(-W, W + 1):
        total = jnp.zeros((rows, left.shape[2], right.shape[3]), jnp.float32)
        for term in range(-W, W + 1):
            other = out_off - term
            if abs(other) > W:
                continue
            total = total + jnp.einsum("nxy,nyz->nxz", left[:, W + term], right[W + term:W + term + rows, W + other], precision=lax.Precision.HIGHEST)
        blocks.append(total * pattern[:, W + out_off].astype(jnp.float32)[:, None, None])
    return jnp.stack(blocks, axis=1)


def reference(density, pattern):
    current = density
    occupancy = []
    for step in range(ITERS):
        extended = jnp.concatenate([current[-W:], current, current[:W]], axis=0)
        square = block_product(current, extended, pattern)
        cube = block_product(square, extended, pattern)
        current = 3.0 * square - 2.0 * cube
        occupancy.append(jnp.einsum("nii->", current[:, W]) / jnp.float32(NB * B))
    return current, jnp.stack(occupancy)
```

```python
import functools

import jax
import jax.numpy as jnp
from jax import lax
from jax.experimental import pallas as pl
from jax.experimental.pallas import tpu as pltpu
from jax.sharding import PartitionSpec as P

MESH = pl.DeviceIdType.MESH
F32 = jnp.float32
BF16 = jnp.bfloat16

B = 128
G, H, M, N = range(4)


def span(first, last):
    return slice(first * 2 * B, (last + 1) * 2 * B)


def block(index):
    return slice(index * B, (index + 1) * B)


def store_split(high, low, at, value):
    top = value.astype(BF16)
    high[at] = top
    low[at] = (value - top.astype(F32)).astype(BF16)


def product(left, right, row, col, first, last):
    (lh, ll), (rh, rl) = left, right
    lat, rat = (span(row, row), span(first, last)), (span(first, last), span(col, col))
    dot = functools.partial(jnp.dot, preferred_element_type=F32)
    return dot(lh[lat], rh[rat]) + dot(lh[lat], rl[rat]) + dot(ll[lat], rh[rat])


def kernel(rows, dens, pat, out, occ, own, halo, dh, dl, sh, sl, s32, eh, el, xs, xr, res, patf, pathalo, tsend, trecv,
           own_send, own_recv, own_loc, halo_send, halo_recv, pat_sem, x_send, x_recv, t_sem, out_sem):
    r, b = lax.axis_index("row"), lax.axis_index("blk")
    devices = 2 * rows
    me = 2 * r + b
    sign = 1 - 2 * b
    half = pl.ds(pl.multiple_of(64 * b, 64), 64)
    other_half = pl.ds(pl.multiple_of(64 * (1 - b), 64), 64)
    after, before = lax.rem(r + 1, rows), lax.rem(r + rows - 1, rows)
    order = F32(4 * rows * B)

    def partner(j):
        p = lax.rem(me + j, devices)
        return {"row": p // 2, "blk": lax.rem(p, 2)}

    barrier = pltpu.get_barrier_semaphore()

    def greet(j, carry):
        pl.semaphore_signal(barrier, inc=1, device_id=partner(j), device_id_type=MESH)
        return carry

    lax.fori_loop(1, devices, greet, 0)
    local = []
    for i in range(4):
        copy = pltpu.make_async_copy(dens.at[i], own.at[i, :, half], own_loc.at[i])
        copy.start()
        local.append(copy)
    patf[...] = jnp.zeros_like(patf)
    patf[0:4, 0:5] = pat[...].astype(F32)
    pl.semaphore_wait(barrier, devices - 1)

    sends = []

    def send(src, dst, send_sem, recv_sem, device):
        copy = pltpu.make_async_remote_copy(src, dst, send_sem, recv_sem, device_id=device, device_id_type=MESH)
        copy.start()
        sends.append(copy)
        return copy

    def send_halo(d):
        n = min(3, 4 - d)
        send(dens.at[d, 2:2 + n], halo.at[d, 2:2 + n, half], halo_send.at[0, d], halo_recv.at[d, b],
             {"row": after, "blk": 0})
        send(dens.at[3 - d, 3 - n:3], halo.at[d, 3 - n:3, half], halo_send.at[1, d], halo_recv.at[d, b],
             {"row": before, "blk": 1})

    pats = send(patf, pathalo, pat_sem.at[0], pat_sem.at[1], {"row": jnp.where(b == 0, after, before), "blk": b})
    send_halo(3)
    send_halo(2)
    theirs = {}
    for q in range(4):
        i = 2 * (1 - b) + q if q < 2 else 2 * b + q - 2
        send(dens.at[i], own.at[i, :, half], own_send.at[q], own_recv.at[i], {"row": r, "blk": 1 - b})
    send_halo(1)
    send_halo(0)

    def wait_own(i):
        pltpu.make_async_copy(dens.at[i], own.at[i, :, half], own_loc.at[i]).wait()
        pltpu.make_async_remote_copy(dens.at[i], own.at[i, :, other_half], own_send.at[0], own_recv.at[i],
                                     device_id={"row": r, "blk": 1 - b}, device_id_type=MESH).wait_recv()

    def wait_halo(d):
        n = min(3, 4 - d)
        start = jnp.where(b == 0, 2, 3 - n)
        for c in range(2):
            at = halo.at[d, pl.ds(start, n), 64 * c:64 * c + 64]
            pltpu.make_async_remote_copy(at, at, halo_send.at[0, d], halo_recv.at[d, c],
                                         device_id={"row": r, "blk": 1 - b}, device_id_type=MESH).wait_recv()

    def own_row(d):
        return jnp.where(b == 0, d - 4, 7 - d)

    D, S, E = (dh, dl), (sh, sl), (eh, el)

    def put(d, e, value):
        store_split(dh, dl, (block(d), block(e)), value)

    def clear(pair, d, e):
        for ref in pair:
            ref[block(d), block(e)] = jnp.zeros((B, B), BF16)

    def mask(d, e):
        ref, i = (pathalo, jnp.where(b == 0, d, 3 - d)) if d < 4 else (patf, own_row(d))
        k = e - d + 2
        return jnp.where(b == 0, ref[pl.ds(i, 1), k:k + 1], ref[pl.ds(i, 1), 4 - k:5 - k])

    def blocks(I, J):
        for a in range(2):
            for c in range(2):
                yield a, c, 2 * I + a, 2 * J + c

    def square(source, I, J, first, last):
        total = product(source, source, I, J, first, last)
        for a, c, d, e in blocks(I, J):
            if abs(d - e) > 2:
                clear(S, d, e)
            else:
                value = total[block(a), block(c)] * mask(d, e)
                s32[block(d), block(e)] = value
                store_split(sh, sl, (block(d), block(e)), value)

    def update(source, I, J, first, last):
        total = product(S, source, I, J, first, last)
        for a, c, d, e in blocks(I, J):
            if abs(d - e) <= 2:
                yield d, e, 3.0 * s32[block(d), block(e)] - 2.0 * (total[block(a), block(c)] * mask(d, e))

    def keep(I, J, first, last):
        for d, e, value in update(D, I, J, first, last):
            store_split(eh, el, (block(d), block(e)), value)
            if d >= 4 and e >= 4:
                xs[e - 4, d - 4] = value
        for a, c, d, e in blocks(I, J):
            if abs(d - e) > 2:
                clear(E, d, e)

    eye = (lax.broadcasted_iota(jnp.int32, (B, B), 0) == lax.broadcasted_iota(jnp.int32, (B, B), 1)).astype(F32)

    def trace(first, second):
        return jnp.sum((first + second) * eye, axis=0, keepdims=True) / order

    for i in range(4):
        wait_own(i)
    for d in range(4, 8):
        for e in range(max(2, d - 2), min(8, d + 3)):
            value = own[own_row(d), 2 + sign * (e - d)]
            put(d, e, value)
            if e < 4:
                put(e, d, value.T)
    for d, e in ((2, 5), (5, 2), (4, 7), (7, 4)):
        clear(D, d, e)
    square(D, M, M, H, N)
    square(D, M, N, M, N)
    keep(M, N, M, N)
    xs[3, 0] = jnp.zeros((B, B), F32)
    other = {"row": r, "blk": 1 - b}
    send(xs.at[2:4], xr.at[2:4], x_send.at[0], x_recv.at[0], other)

    def put_halo(d):
        for k in range(min(3, 4 - d)):
            value = halo[d, 2 + sign * k]
            put(d, d + k, value)
            if k:
                put(d + k, d, value.T)

    wait_halo(3)
    put_halo(3)
    wait_halo(2)
    put_halo(2)
    square(D, M, H, H, M)
    keep(M, M, H, N)
    send(xs.at[0:2], xr.at[0:2], x_send.at[1], x_recv.at[1], other)
    tsend[...] = jnp.zeros_like(tsend)
    tsend[0:1, :] = trace(xs[0, 0], xs[1, 1])
    keep(M, H, H, M)
    pats.wait_recv()
    square(D, H, M, H, M)

    wait_halo(1)
    put_halo(1)
    wait_halo(0)
    put_halo(0)
    clear(D, 0, 3)
    clear(D, 3, 0)
    square(D, H, G, G, H)
    square(D, H, H, G, M)
    keep(H, H, G, M)
    keep(H, M, H, M)

    for part, at in ((0, slice(2, 4)), (1, slice(0, 2))):
        pltpu.make_async_remote_copy(xs.at[at], xr.at[at], x_send.at[part], x_recv.at[part], device_id=other,
                                     device_id_type=MESH).wait_recv()
    for a in range(2):
        for c in range(4):
            store_split(eh, el, (block(6 + a), block(4 + c)), xr[3 - c, 1 - a])
    square(E, M, M, H, N)
    square(E, M, H, H, M)
    square(E, M, N, M, N)

    def finish(J, first, last):
        kept = []
        for d, e, value in update(E, M, J, first, last):
            res[jnp.where(b == 0, d - 4, 5 - d), 2 + sign * (e - d)] = value
            if d == e:
                kept.append(value)
        return kept

    tsend[1:2, :] = trace(*finish(M, H, N))

    def tell(j, carry):
        pltpu.make_async_remote_copy(tsend, trecv.at[me], t_sem.at[0], t_sem.at[1], device_id=partner(j),
                                     device_id_type=MESH).start()
        return carry

    lax.fori_loop(1, devices, tell, 0)
    finish(H, H, M)
    finish(N, M, N)
    mine = pltpu.make_async_copy(res.at[:, :, half], out.at[pl.ds(2 * b, 2)], out_sem.at[0])
    mine.start()
    yours = pltpu.make_async_remote_copy(res.at[:, :, other_half], out.at[pl.ds(2 * b, 2)], out_sem.at[1],
                                         out_sem.at[2], device_id=other, device_id_type=MESH)
    yours.start()
    all_but_one = trecv.at[0:devices - 1]
    told = pltpu.make_async_remote_copy(all_but_one, all_but_one, t_sem.at[0], t_sem.at[1], device_id=other,
                                        device_id_type=MESH)
    told.wait_recv()
    trecv[me] = tsend[...]
    total = jnp.sum(trecv[...], axis=0)
    occ[0] = jnp.sum(total[0:1, :])
    occ[1] = jnp.sum(total[1:2, :])
    told.wait_send()
    for copy in sends:
        copy.wait_send()
    mine.wait()
    yours.wait()


def local(density, pattern):
    rows = lax.axis_size("row")
    dma = pltpu.SemaphoreType.DMA
    wide = 8 * B
    return pl.pallas_call(
        functools.partial(kernel, rows),
        out_shape=(jax.ShapeDtypeStruct(density.shape, F32), jax.ShapeDtypeStruct((2,), F32)),
        in_specs=[pl.BlockSpec(memory_space=pl.ANY), pl.BlockSpec(memory_space=pltpu.VMEM)],
        out_specs=(pl.BlockSpec(memory_space=pl.ANY), pl.BlockSpec(memory_space=pltpu.SMEM)),
        scratch_shapes=[
            pltpu.VMEM((4, 5, B, B), F32),
            pltpu.VMEM((4, 5, B, B), F32),
            pltpu.VMEM((wide, wide), BF16),
            pltpu.VMEM((wide, wide), BF16),
            pltpu.VMEM((wide, wide), BF16),
            pltpu.VMEM((wide, wide), BF16),
            pltpu.VMEM((wide, wide), F32),
            pltpu.VMEM((wide, wide), BF16),
            pltpu.VMEM((wide, wide), BF16),
            pltpu.VMEM((4, 2, B, B), F32),
            pltpu.VMEM((4, 2, B, B), F32),
            pltpu.VMEM((2, 5, B, B), F32),
            pltpu.VMEM((8, B), F32),
            pltpu.VMEM((8, B), F32),
            pltpu.VMEM((8, B), F32),
            pltpu.VMEM((2 * rows, 8, B), F32),
            dma((4,)), dma((4,)), dma((4,)), dma((2, 4)), dma((4, 2)), dma((2,)), dma((2,)), dma((2,)), dma((2,)),
            dma((3,)),
        ],
        compiler_params=pltpu.CompilerParams(collective_id=0, has_side_effects=True, vmem_limit_bytes=40 * 2**20),
        cost_estimate=pl.CostEstimate(flops=4 * 10**9, bytes_accessed=4 * 10**6, transcendentals=0),
    )(density, pattern)


def solution(mesh):
    placed = (P(("grp", "row"), None, "blk", None), P(("grp", "row"), None))
    return jax.shard_map(
        local,
        mesh=mesh,
        in_specs=placed,
        out_specs=(P(("grp", "row"), None, "blk", None), P("grp")),
        check_vma=False,
    )
```

```python
import functools

import jax
import jax.numpy as jnp
from jax import lax
from jax.experimental import pallas as pl
from jax.experimental.pallas import tpu as pltpu
from jax.sharding import PartitionSpec as P

MESH = pl.DeviceIdType.MESH
F32 = jnp.float32
BF16 = jnp.bfloat16

B = 128
G, H, M, N = range(4)
CHUNKS = ((0, 0, 2), (1, 0, 1), (3, 0, 1), (2, 0, 2), (1, 1, 2), (0, 2, 1))
VMEM_BYTES = 40 * 2**20


def span(first, last):
    return slice(first * 2 * B, (last + 1) * 2 * B)


def block(index):
    return slice(index * B, (index + 1) * B)


def store_split(high, low, at, value):
    top = value.astype(BF16)
    high[at] = top
    low[at] = (value - top.astype(F32)).astype(BF16)


def product(left, right, row, col, first, last):
    (lh, ll), (rh, rl) = left, right
    lat, rat = (span(row, row), span(first, last)), (span(first, last), span(col, col))
    dot = functools.partial(jnp.dot, preferred_element_type=F32)
    return dot(lh[lat], rh[rat]) + dot(lh[lat], rl[rat]) + dot(ll[lat], rh[rat])


def kernel(rows, dens, pat, out, occ, own, halo, dh, dl, sh, sl, s32, eh, el, xs, xr, res, pati, patf, pathalo, tsend, trecv,
           own_send, own_recv, own_loc, halo_send, halo_recv, relay_send,
           relay_recv, pat_sem, x_send, x_recv, t_sem, out_sem):
    r, b = lax.axis_index("row"), lax.axis_index("blk")
    devices = 2 * rows
    me = 2 * r + b
    sign = 1 - 2 * b
    half = pl.ds(pl.multiple_of(64 * b, 64), 64)
    other_half = pl.ds(pl.multiple_of(64 * (1 - b), 64), 64)
    after, before = lax.rem(r + 1, rows), lax.rem(r + rows - 1, rows)
    order = F32(4 * rows * B)

    def partner(j):
        p = lax.rem(me + j, devices)
        return {"row": p // 2, "blk": lax.rem(p, 2)}

    barrier = pltpu.get_barrier_semaphore()

    def greet(j, carry):
        pl.semaphore_signal(barrier, inc=1, device_id=partner(j), device_id_type=MESH)
        return carry

    lax.fori_loop(1, devices, greet, 0)
    pat_in = pltpu.make_async_copy(pat, pati, pat_sem.at[2])
    pat_in.start()
    local = []
    for i in range(4):
        copy = pltpu.make_async_copy(dens.at[i], own.at[i, :, half], own_loc.at[i])
        copy.start()
        local.append(copy)
    patf[...] = jnp.zeros_like(patf)
    pat_in.wait()
    patf[0:4, 0:5] = pati[...].astype(F32)
    pl.semaphore_wait(barrier, devices - 1)

    sends = []

    def send(src, dst, send_sem, recv_sem, device):
        copy = pltpu.make_async_remote_copy(src, dst, send_sem, recv_sem, device_id=device, device_id_type=MESH)
        copy.start()
        sends.append(copy)
        return copy

    even = lax.rem(r, 2) == 0
    toward = jnp.where(even, 1, -1)
    direct = lax.rem(r + b, 2) == 1
    relay_to = {"row": lax.rem(r + 4 * b - 2 + rows, rows), "blk": 1 - b}

    def chunk_at(ref, side, c, *rest):
        d, k, n = CHUNKS[c]
        return ref.at[(d, pl.ds(jnp.where(side == 1, 2 + k, 3 - k - n), n)) + rest]

    def send_halo(c):
        d, k, n = CHUNKS[c]
        i = jnp.where(even, d, 3 - d)
        start = jnp.where(even, 2 + k, 3 - k - n)
        send(dens.at[i, pl.ds(start, n)], chunk_at(halo, toward, c, half), halo_send.at[c], halo_recv.at[c, b],
             {"row": lax.rem(r + toward + rows, rows), "blk": jnp.where(even, 0, 1)})

    pats = send(patf, pathalo, pat_sem.at[0], pat_sem.at[1], {"row": jnp.where(b == 0, after, before), "blk": b})
    for c in range(3):
        send_halo(c)
    for q in range(4):
        i = 2 * (1 - b) + q if q < 2 else 2 * b + q - 2
        send(dens.at[i], own.at[i, :, half], own_send.at[q], own_recv.at[i], {"row": r, "blk": 1 - b})
    for c in range(3, len(CHUNKS)):
        send_halo(c)

    def wait_own(i):
        pltpu.make_async_copy(dens.at[i], own.at[i, :, half], own_loc.at[i]).wait()
        pltpu.make_async_remote_copy(dens.at[i], own.at[i, :, other_half], own_send.at[0], own_recv.at[i],
                                     device_id={"row": r, "blk": 1 - b}, device_id_type=MESH).wait_recv()

    def relay(c):
        at = chunk_at(halo, sign, c)
        return pltpu.make_async_remote_copy(at, at, relay_send.at[c], relay_recv.at[c], device_id=relay_to,
                                            device_id_type=MESH)

    def wait_direct(*chunks):
        @pl.when(direct)
        def _():
            for c in chunks:
                for h in range(2):
                    at = chunk_at(halo, sign, c, pl.ds(64 * h, 64))
                    pltpu.make_async_remote_copy(at, at, halo_send.at[c], halo_recv.at[c, h], device_id=relay_to,
                                                 device_id_type=MESH).wait_recv()
                relay(c).start()

    def wait_relayed(*chunks):
        @pl.when(jnp.logical_not(direct))
        def _():
            for c in chunks:
                at = chunk_at(halo, -sign, c)
                pltpu.make_async_remote_copy(at, at, relay_send.at[c], relay_recv.at[c], device_id=relay_to,
                                             device_id_type=MESH).wait_recv()

    def own_row(d):
        return jnp.where(b == 0, d - 4, 7 - d)

    D, S, E = (dh, dl), (sh, sl), (eh, el)

    def put(d, e, value):
        store_split(dh, dl, (block(d), block(e)), value)

    def clear(pair, d, e):
        for ref in pair:
            ref[block(d), block(e)] = jnp.zeros((B, B), BF16)

    def mask(d, e):
        ref, i = (pathalo, jnp.where(b == 0, d, 3 - d)) if d < 4 else (patf, own_row(d))
        k = e - d + 2
        return jnp.where(b == 0, ref[pl.ds(i, 1), k:k + 1], ref[pl.ds(i, 1), 4 - k:5 - k])

    def blocks(I, J):
        for a in range(2):
            for c in range(2):
                yield a, c, 2 * I + a, 2 * J + c

    def square(source, I, J, first, last):
        total = product(source, source, I, J, first, last)
        for a, c, d, e in blocks(I, J):
            if abs(d - e) > 2:
                clear(S, d, e)
            else:
                value = total[block(a), block(c)] * mask(d, e)
                s32[block(d), block(e)] = value
                store_split(sh, sl, (block(d), block(e)), value)

    def update(source, I, J, first, last):
        total = product(S, source, I, J, first, last)
        for a, c, d, e in blocks(I, J):
            if abs(d - e) <= 2:
                yield d, e, 3.0 * s32[block(d), block(e)] - 2.0 * (total[block(a), block(c)] * mask(d, e))

    def keep(I, J, first, last):
        for d, e, value in update(D, I, J, first, last):
            store_split(eh, el, (block(d), block(e)), value)
            if d >= 4 and e >= 4:
                xs[e - 4, d - 4] = value
        for a, c, d, e in blocks(I, J):
            if abs(d - e) > 2:
                clear(E, d, e)

    eye = (lax.broadcasted_iota(jnp.int32, (B, B), 0) == lax.broadcasted_iota(jnp.int32, (B, B), 1)).astype(F32)

    def trace(first, second):
        return jnp.sum((first + second) * eye, axis=0, keepdims=True) / order

    for i in range(4):
        wait_own(i)
    for d in range(4, 8):
        for e in range(max(2, d - 2), min(8, d + 3)):
            value = own[own_row(d), 2 + sign * (e - d)]
            put(d, e, value)
            if e < 4:
                put(e, d, value.T)
    for d, e in ((2, 5), (5, 2), (4, 7), (7, 4)):
        clear(D, d, e)
    wait_direct(0)
    square(D, M, M, H, N)
    square(D, M, N, M, N)
    wait_direct(1)
    keep(M, N, M, N)
    xs[3, 0] = jnp.zeros((B, B), F32)
    other = {"row": r, "blk": 1 - b}
    send(xs.at[2:4], xr.at[2:4], x_send.at[0], x_recv.at[0], other)

    def put_halo(d, k):
        value = halo[jnp.where(direct, d, 3 - d - k), 2 + sign * k * jnp.where(direct, 1, -1)]
        if k == 0:
            put(d, d, value)
        else:
            turned = value.T
            put(d, d + k, jnp.where(direct, value, turned))
            put(d + k, d, jnp.where(direct, turned, value))

    wait_direct(2, 3)
    wait_relayed(0, 1)
    put_halo(3, 0)
    put_halo(2, 0)
    put_halo(2, 1)
    square(D, M, H, H, M)
    keep(M, M, H, N)
    send(xs.at[0:2], xr.at[0:2], x_send.at[1], x_recv.at[1], other)
    tsend[...] = jnp.zeros_like(tsend)
    tsend[0:1, :] = trace(xs[0, 0], xs[1, 1])
    wait_direct(4)
    keep(M, H, H, M)
    pats.wait_recv()
    square(D, H, M, H, M)

    wait_direct(5)
    wait_relayed(2, 3, 4, 5)
    for d, k in ((0, 0), (0, 1), (0, 2), (1, 0), (1, 1), (1, 2)):
        put_halo(d, k)
    clear(D, 0, 3)
    clear(D, 3, 0)
    square(D, H, G, G, H)
    square(D, H, H, G, M)
    keep(H, H, G, M)
    keep(H, M, H, M)

    for part, at in ((0, slice(2, 4)), (1, slice(0, 2))):
        pltpu.make_async_remote_copy(xs.at[at], xr.at[at], x_send.at[part], x_recv.at[part], device_id=other,
                                     device_id_type=MESH).wait_recv()
    for a in range(2):
        for c in range(4):
            store_split(eh, el, (block(6 + a), block(4 + c)), xr[3 - c, 1 - a])
    square(E, M, M, H, N)
    square(E, M, H, H, M)
    square(E, M, N, M, N)

    def finish(J, first, last):
        kept = []
        for d, e, value in update(E, M, J, first, last):
            res[jnp.where(b == 0, d - 4, 5 - d), 2 + sign * (e - d)] = value
            if d == e:
                kept.append(value)
        return kept

    tsend[1:2, :] = trace(*finish(M, H, N))

    def tell(j, carry):
        pltpu.make_async_remote_copy(tsend, trecv.at[me], t_sem.at[0], t_sem.at[1], device_id=partner(j),
                                     device_id_type=MESH).start()
        return carry

    lax.fori_loop(1, devices, tell, 0)
    finish(H, H, M)
    finish(N, M, N)
    mine = pltpu.make_async_copy(res.at[:, :, half], out.at[pl.ds(2 * b, 2)], out_sem.at[0])
    mine.start()
    yours = pltpu.make_async_remote_copy(res.at[:, :, other_half], out.at[pl.ds(2 * b, 2)], out_sem.at[1],
                                         out_sem.at[2], device_id=other, device_id_type=MESH)
    yours.start()
    all_but_one = trecv.at[0:devices - 1]
    told = pltpu.make_async_remote_copy(all_but_one, all_but_one, t_sem.at[0], t_sem.at[1], device_id=other,
                                        device_id_type=MESH)
    told.wait_recv()
    trecv[me] = tsend[...]
    total = jnp.sum(trecv[...], axis=0)
    occ[0] = jnp.sum(total[0:1, :])
    occ[1] = jnp.sum(total[1:2, :])
    told.wait_send()

    @pl.when(direct)
    def _():
        for c in range(len(CHUNKS)):
            relay(c).wait_send()

    for copy in sends:
        copy.wait_send()
    mine.wait()
    yours.wait()


def local(density, pattern):
    rows = lax.axis_size("row")
    dma = pltpu.SemaphoreType.DMA
    wide = 8 * B
    return pl.pallas_call(
        functools.partial(kernel, rows),
        out_shape=(jax.ShapeDtypeStruct(density.shape, F32), jax.ShapeDtypeStruct((2,), F32)),
        in_specs=[pl.BlockSpec(memory_space=pltpu.HBM), pl.BlockSpec(memory_space=pltpu.HBM)],
        out_specs=(pl.BlockSpec(memory_space=pl.ANY), pl.BlockSpec(memory_space=pltpu.SMEM)),
        scratch_shapes=[
            pltpu.VMEM((4, 5, B, B), F32),
            pltpu.VMEM((4, 5, B, B), F32),
            pltpu.VMEM((wide, wide), BF16),
            pltpu.VMEM((wide, wide), BF16),
            pltpu.VMEM((wide, wide), BF16),
            pltpu.VMEM((wide, wide), BF16),
            pltpu.VMEM((wide, wide), F32),
            pltpu.VMEM((wide, wide), BF16),
            pltpu.VMEM((wide, wide), BF16),
            pltpu.VMEM((4, 2, B, B), F32),
            pltpu.VMEM((4, 2, B, B), F32),
            pltpu.VMEM((2, 5, B, B), F32),
            pltpu.VMEM((4, 5), jnp.int32),
            pltpu.VMEM((8, B), F32),
            pltpu.VMEM((8, B), F32),
            pltpu.VMEM((8, B), F32),
            pltpu.VMEM((2 * rows, 8, B), F32),
            dma((4,)), dma((4,)), dma((4,)), dma((6,)), dma((6, 2)), dma((6,)), dma((6,)), dma((3,)), dma((2,)), dma((2,)), dma((2,)),
            dma((3,)),
        ],
        compiler_params=pltpu.CompilerParams(collective_id=0, has_side_effects=True, vmem_limit_bytes=VMEM_BYTES),
        cost_estimate=pl.CostEstimate(flops=4 * 10**9, bytes_accessed=4 * 10**6, transcendentals=0),
    )(pltpu.with_memory_space_constraint(density, pltpu.HBM), pltpu.with_memory_space_constraint(pattern, pltpu.HBM))


def solution(mesh):
    placed = (P(("grp", "row"), None, "blk", None), P(("grp", "row"), None))
    return jax.shard_map(
        local,
        mesh=mesh,
        in_specs=placed,
        out_specs=(P(("grp", "row"), None, "blk", None), P("grp")),
        check_vma=False,
    )
```

```python
import functools

import jax
import jax.numpy as jnp
from jax import lax
from jax.experimental import pallas as pl
from jax.experimental.pallas import tpu as pltpu
from jax.sharding import PartitionSpec as P

MESH = pl.DeviceIdType.MESH
F32 = jnp.float32
BF16 = jnp.bfloat16

B = 128
G, H, M, N = range(4)
CHUNKS = ((0, 0, 2), (1, 0, 1), (3, 0, 1), (2, 0, 2), (1, 1, 2), (0, 2, 1))
RELAYED = 4
VMEM_BYTES = 40 * 2**20


def span(first, last):
    return slice(first * 2 * B, (last + 1) * 2 * B)


def block(index):
    return slice(index * B, (index + 1) * B)


def store_split(high, low, at, value):
    top = value.astype(BF16)
    high[at] = top
    low[at] = (value - top.astype(F32)).astype(BF16)


def product(left, right, row, col, first, last):
    (lh, ll), (rh, rl) = left, right
    lat, rat = (span(row, row), span(first, last)), (span(first, last), span(col, col))
    dot = functools.partial(jnp.dot, preferred_element_type=F32)
    return dot(lh[lat], rh[rat]) + dot(lh[lat], rl[rat]) + dot(ll[lat], rh[rat])


def kernel(rows, dens, pat, out, occ, own, halo, dh, dl, sh, sl, s32, eh, el, xs, xr, res, pati, patf, pathalo, tsend, trecv,
           own_send, own_recv, own_loc, halo_send, halo_recv, relay_send,
           relay_recv, pat_sem, x_send, x_recv, t_sem, out_sem):
    r, b = lax.axis_index("row"), lax.axis_index("blk")
    devices = 2 * rows
    me = 2 * r + b
    sign = 1 - 2 * b
    half = pl.ds(pl.multiple_of(64 * b, 64), 64)
    other_half = pl.ds(pl.multiple_of(64 * (1 - b), 64), 64)
    after, before = lax.rem(r + 1, rows), lax.rem(r + rows - 1, rows)
    order = F32(4 * rows * B)

    def partner(j):
        p = lax.rem(me + j, devices)
        return {"row": p // 2, "blk": lax.rem(p, 2)}

    barrier = pltpu.get_barrier_semaphore()

    def greet(j, carry):
        pl.semaphore_signal(barrier, inc=1, device_id=partner(j), device_id_type=MESH)
        return carry

    lax.fori_loop(1, devices, greet, 0)
    pat_in = pltpu.make_async_copy(pat, pati, pat_sem.at[2])
    pat_in.start()
    local = []
    for i in range(4):
        copy = pltpu.make_async_copy(dens.at[i], own.at[i, :, half], own_loc.at[i])
        copy.start()
        local.append(copy)
    patf[...] = jnp.zeros_like(patf)
    pat_in.wait()
    patf[0:4, 0:5] = pati[...].astype(F32)
    pl.semaphore_wait(barrier, devices - 1)

    sends = []

    def start_copy(src, dst, send_sem, recv_sem, device):
        copy = pltpu.make_async_remote_copy(src, dst, send_sem, recv_sem, device_id=device, device_id_type=MESH)
        copy.start()
        return copy

    def send(*what):
        copy = start_copy(*what)
        sends.append(copy)
        return copy

    even = lax.rem(r, 2) == 0
    toward = jnp.where(even, 1, -1)
    direct = lax.rem(r + b, 2) == 1
    relay_to = {"row": lax.rem(r + 4 * b - 2 + rows, rows), "blk": 1 - b}

    def chunk_at(ref, side, c, *rest):
        d, k, n = CHUNKS[c]
        return ref.at[(d, pl.ds(jnp.where(side == 1, 2 + k, 3 - k - n), n)) + rest]

    def send_halo(c):
        d, k, n = CHUNKS[c]
        i = jnp.where(even, d, 3 - d)
        start = jnp.where(even, 2 + k, 3 - k - n)
        for q, step in enumerate((toward, -toward)[:1 if c < RELAYED else 2]):
            start_copy(dens.at[i, pl.ds(start, n)], chunk_at(halo, toward, c, half), halo_send.at[q, c], halo_recv.at[c, b],
                 {"row": lax.rem(r + step + rows, rows), "blk": jnp.where(step == 1, 0, 1)})

    pats = send(patf, pathalo, pat_sem.at[0], pat_sem.at[1], {"row": jnp.where(b == 0, after, before), "blk": b})
    send_halo(0)
    send_halo(1)
    for q in range(4):
        i = 2 * (1 - b) + q if q < 2 else 2 * b + q - 2
        send(dens.at[i], own.at[i, :, half], own_send.at[q], own_recv.at[i], {"row": r, "blk": 1 - b})

    def second(c):
        pltpu.make_async_remote_copy(chunk_at(halo, sign, c, half), chunk_at(halo, sign, c, half), halo_send.at[1, c],
                                     halo_recv.at[c, b], device_id=relay_to, device_id_type=MESH).wait_send()

    def sent(c):
        pltpu.make_async_remote_copy(chunk_at(halo, sign, c, half), chunk_at(halo, sign, c, half), halo_send.at[0, c],
                                     halo_recv.at[c, b], device_id=relay_to, device_id_type=MESH).wait_send()


    def wait_own(i):
        pltpu.make_async_copy(dens.at[i], own.at[i, :, half], own_loc.at[i]).wait()
        pltpu.make_async_remote_copy(dens.at[i], own.at[i, :, other_half], own_send.at[0], own_recv.at[i],
                                     device_id={"row": r, "blk": 1 - b}, device_id_type=MESH).wait_recv()

    def relay(c):
        at = chunk_at(halo, sign, c)
        return pltpu.make_async_remote_copy(at, at, relay_send.at[c], relay_recv.at[c], device_id=relay_to,
                                            device_id_type=MESH)

    def wait_halves(c, side):
        for h in range(2):
            at = chunk_at(halo, side, c, pl.ds(64 * h, 64))
            pltpu.make_async_remote_copy(at, at, halo_send.at[0, c], halo_recv.at[c, h], device_id=relay_to,
                                         device_id_type=MESH).wait_recv()

    def wait_direct(*chunks):
        @pl.when(direct)
        def _():
            for c in chunks:
                wait_halves(c, sign)
                if c < RELAYED:
                    relay(c).start()

    def wait_relayed(*chunks):
        @pl.when(jnp.logical_not(direct))
        def _():
            for c in chunks:
                if c < RELAYED:
                    at = chunk_at(halo, -sign, c)
                    pltpu.make_async_remote_copy(at, at, relay_send.at[c], relay_recv.at[c], device_id=relay_to,
                                                 device_id_type=MESH).wait_recv()
                else:
                    wait_halves(c, -sign)

    def own_row(d):
        return jnp.where(b == 0, d - 4, 7 - d)

    D, S, E = (dh, dl), (sh, sl), (eh, el)

    def put(d, e, value):
        store_split(dh, dl, (block(d), block(e)), value)

    def clear(pair, d, e):
        for ref in pair:
            ref[block(d), block(e)] = jnp.zeros((B, B), BF16)

    def mask(d, e):
        ref, i = (pathalo, jnp.where(b == 0, d, 3 - d)) if d < 4 else (patf, own_row(d))
        k = e - d + 2
        return jnp.where(b == 0, ref[pl.ds(i, 1), k:k + 1], ref[pl.ds(i, 1), 4 - k:5 - k])

    def blocks(I, J):
        for a in range(2):
            for c in range(2):
                yield a, c, 2 * I + a, 2 * J + c

    def square(source, I, J, first, last):
        total = product(source, source, I, J, first, last)
        for a, c, d, e in blocks(I, J):
            if abs(d - e) > 2:
                clear(S, d, e)
            else:
                value = total[block(a), block(c)] * mask(d, e)
                s32[block(d), block(e)] = value
                store_split(sh, sl, (block(d), block(e)), value)

    def update(source, I, J, first, last):
        total = product(S, source, I, J, first, last)
        for a, c, d, e in blocks(I, J):
            if abs(d - e) <= 2:
                yield d, e, 3.0 * s32[block(d), block(e)] - 2.0 * (total[block(a), block(c)] * mask(d, e))

    def keep(I, J, first, last):
        for d, e, value in update(D, I, J, first, last):
            store_split(eh, el, (block(d), block(e)), value)
            if d >= 4 and e >= 4:
                xs[e - 4, d - 4] = value
        for a, c, d, e in blocks(I, J):
            if abs(d - e) > 2:
                clear(E, d, e)

    eye = (lax.broadcasted_iota(jnp.int32, (B, B), 0) == lax.broadcasted_iota(jnp.int32, (B, B), 1)).astype(F32)

    def trace(first, second):
        return jnp.sum((first + second) * eye, axis=0, keepdims=True) / order

    for i in range(4):
        wait_own(i)
    sent(0)
    send_halo(2)
    for d in range(4, 8):
        for e in range(max(2, d - 2), min(8, d + 3)):
            value = own[own_row(d), 2 + sign * (e - d)]
            put(d, e, value)
            if e < 4:
                put(e, d, value.T)
    for d, e in ((2, 5), (5, 2), (4, 7), (7, 4)):
        clear(D, d, e)
    wait_direct(0)
    sent(1)
    send_halo(3)
    square(D, M, M, H, N)
    sent(2)
    send_halo(4)
    wait_direct(1)
    square(D, M, N, M, N)
    sent(3)
    send_halo(5)
    keep(M, N, M, N)
    xs[3, 0] = jnp.zeros((B, B), F32)
    other = {"row": r, "blk": 1 - b}
    send(xs.at[2:4], xr.at[2:4], x_send.at[0], x_recv.at[0], other)

    def put_halo(d, k):
        value = halo[jnp.where(direct, d, 3 - d - k), 2 + sign * k * jnp.where(direct, 1, -1)]
        if k == 0:
            put(d, d, value)
        else:
            turned = value.T
            put(d, d + k, jnp.where(direct, value, turned))
            put(d + k, d, jnp.where(direct, turned, value))

    wait_direct(2, 3)
    wait_relayed(0, 1)
    put_halo(3, 0)
    put_halo(2, 0)
    put_halo(2, 1)
    square(D, M, H, H, M)
    keep(M, M, H, N)
    send(xs.at[0:2], xr.at[0:2], x_send.at[1], x_recv.at[1], other)
    tsend[...] = jnp.zeros_like(tsend)
    tsend[0:1, :] = trace(xs[0, 0], xs[1, 1])
    keep(M, H, H, M)
    pats.wait_recv()
    square(D, H, M, H, M)

    wait_direct(4, 5)
    wait_relayed(2, 3, 4, 5)
    for d, k in ((0, 0), (0, 1), (0, 2), (1, 0), (1, 1), (1, 2)):
        put_halo(d, k)
    clear(D, 0, 3)
    clear(D, 3, 0)
    square(D, H, G, G, H)
    square(D, H, H, G, M)
    keep(H, H, G, M)
    keep(H, M, H, M)

    for part, at in ((0, slice(2, 4)), (1, slice(0, 2))):
        pltpu.make_async_remote_copy(xs.at[at], xr.at[at], x_send.at[part], x_recv.at[part], device_id=other,
                                     device_id_type=MESH).wait_recv()
    for a in range(2):
        for c in range(4):
            store_split(eh, el, (block(6 + a), block(4 + c)), xr[3 - c, 1 - a])
    square(E, M, M, H, N)
    square(E, M, H, H, M)
    square(E, M, N, M, N)

    def finish(J, first, last):
        kept = []
        for d, e, value in update(E, M, J, first, last):
            res[jnp.where(b == 0, d - 4, 5 - d), 2 + sign * (e - d)] = value
            if d == e:
                kept.append(value)
        return kept

    tsend[1:2, :] = trace(*finish(M, H, N))

    def tell(j, carry):
        pltpu.make_async_remote_copy(tsend, trecv.at[me], t_sem.at[0], t_sem.at[1], device_id=partner(j),
                                     device_id_type=MESH).start()
        return carry

    lax.fori_loop(1, devices, tell, 0)
    finish(H, H, M)
    finish(N, M, N)
    mine = pltpu.make_async_copy(res.at[:, :, half], out.at[pl.ds(2 * b, 2)], out_sem.at[0])
    mine.start()
    yours = pltpu.make_async_remote_copy(res.at[:, :, other_half], out.at[pl.ds(2 * b, 2)], out_sem.at[1],
                                         out_sem.at[2], device_id=other, device_id_type=MESH)
    yours.start()
    all_but_one = trecv.at[0:devices - 1]
    told = pltpu.make_async_remote_copy(all_but_one, all_but_one, t_sem.at[0], t_sem.at[1], device_id=other,
                                        device_id_type=MESH)
    told.wait_recv()
    trecv[me] = tsend[...]
    total = jnp.sum(trecv[...], axis=0)
    occ[0] = jnp.sum(total[0:1, :])
    occ[1] = jnp.sum(total[1:2, :])
    told.wait_send()

    @pl.when(direct)
    def _():
        for c in range(RELAYED):
            relay(c).wait_send()

    for copy in sends:
        copy.wait_send()
    for c in range(4, len(CHUNKS)):
        sent(c)
        second(c)
    mine.wait()
    yours.wait()


def local(density, pattern):
    rows = lax.axis_size("row")
    dma = pltpu.SemaphoreType.DMA
    wide = 8 * B
    return pl.pallas_call(
        functools.partial(kernel, rows),
        out_shape=(jax.ShapeDtypeStruct(density.shape, F32), jax.ShapeDtypeStruct((2,), F32)),
        in_specs=[pl.BlockSpec(memory_space=pltpu.HBM), pl.BlockSpec(memory_space=pltpu.HBM)],
        out_specs=(pl.BlockSpec(memory_space=pl.ANY), pl.BlockSpec(memory_space=pltpu.SMEM)),
        scratch_shapes=[
            pltpu.VMEM((4, 5, B, B), F32),
            pltpu.VMEM((4, 5, B, B), F32),
            pltpu.VMEM((wide, wide), BF16),
            pltpu.VMEM((wide, wide), BF16),
            pltpu.VMEM((wide, wide), BF16),
            pltpu.VMEM((wide, wide), BF16),
            pltpu.VMEM((wide, wide), F32),
            pltpu.VMEM((wide, wide), BF16),
            pltpu.VMEM((wide, wide), BF16),
            pltpu.VMEM((4, 2, B, B), F32),
            pltpu.VMEM((4, 2, B, B), F32),
            pltpu.VMEM((2, 5, B, B), F32),
            pltpu.VMEM((4, 5), jnp.int32),
            pltpu.VMEM((8, B), F32),
            pltpu.VMEM((8, B), F32),
            pltpu.VMEM((8, B), F32),
            pltpu.VMEM((2 * rows, 8, B), F32),
            dma((4,)), dma((4,)), dma((4,)), dma((2, 6)), dma((6, 2)), dma((RELAYED,)), dma((RELAYED,)), dma((3,)), dma((2,)), dma((2,)), dma((2,)),
            dma((3,)),
        ],
        compiler_params=pltpu.CompilerParams(collective_id=0, has_side_effects=True, vmem_limit_bytes=VMEM_BYTES),
        cost_estimate=pl.CostEstimate(flops=4 * 10**9, bytes_accessed=4 * 10**6, transcendentals=0),
    )(pltpu.with_memory_space_constraint(density, pltpu.HBM), pltpu.with_memory_space_constraint(pattern, pltpu.HBM))


def solution(mesh):
    placed = (P(("grp", "row"), None, "blk", None), P(("grp", "row"), None))
    return jax.shard_map(
        local,
        mesh=mesh,
        in_specs=placed,
        out_specs=(P(("grp", "row"), None, "blk", None), P("grp")),
        check_vma=False,
    )
```
